256 devices in a mesh: sec: 32 (over y, x, core), mpo: 8 (over z).
Axes of the slice: x: 4, y: 4, z: 8, core: 2. Of those that a mesh axis runs over, the one named last changes fastest.
Arguments:
- trial: bfloat16 [2, 768, 128, 128], P(None, 'sec'), may hold values from -6 to 6
- left_env: bfloat16 [24, 1024, 128, 128], P('mpo', 'sec'), may hold values from -0.5 to 0.5
- right_env: bfloat16 [24, 1024, 128, 128], P('mpo', 'sec'), may hold values from -0.109375 to 0.109375
- left_slot: int32 [768], P('sec'), may hold values from 0 to 31
- dest: int32 [768, 1], P('sec'), may hold values from 0 to 31, as said below
- right_slot: int32 [768], P('sec'), may hold values from 0 to 31
Outputs:
- applied: bfloat16 [2048, 2, 128, 128], P(('sec', 'mpo'))
The draws below stay inside these ranges and needn't reach their ends.
Inputs may be any that keep to these rules, and one draw needn't show every extreme that they name: `dest`: on the rows of one device no destination appears more than 2 times; in every draw one destination, the same for all devices, appears exactly 2 times on every device.
All inputs are finite; a program needn't handle non-finite values.
Results may differ from the reference program's by a relative error of at most 0.017.
Values may be sent and summed in bfloat16 or wider, within the bound.
A program may use at most 128 MiB of HBM per device.

```python
import jax
import jax.numpy as jnp
from jax import lax

BLK = 128
MB_DEV = 3
NL_DEV = 32
NR_DEV = 32
NB_DEV = 24
MB = 24
NL = 1024
NR = 1024
NB = 768
CAP = 2
RECV = 2048
N_SEC = 32
N_MPO = 8


def draw_dest(key, part):
    hot_dest = jax.random.randint(jax.random.fold_in(key, 7), (), 0, N_SEC)
    dest_pool = jnp.repeat(jnp.arange(N_SEC, dtype=jnp.int32), CAP)
    pool_size = N_SEC * CAP

    def per_device(dev_key):
        shuffled = jax.random.permutation(jax.random.fold_in(dev_key, 1), pool_size).astype(jnp.int32)
        priority = shuffled + jnp.where(dest_pool == hot_dest, 0, pool_size).astype(jnp.int32)
        picked_dests = dest_pool[jnp.argsort(priority, stable=True)][:NB_DEV]
        return jax.random.permutation(jax.random.fold_in(dev_key, 2), picked_dests)
    device_keys = jax.vmap(lambda device_number: jax.random.fold_in(key, device_number))(jnp.arange(N_SEC))
    return jax.vmap(per_device)(device_keys).reshape(NB_DEV * N_SEC, 1).astype(jnp.int32)


def with_ends(array, key, low, top_value):
    longest = array.shape.index(max(array.shape))
    spots = []
    for shift in (0, 1):
        where = [jax.random.randint(jax.random.fold_in(key, axis), (), 0, length) for axis, length in enumerate(array.shape)]
        where[longest] = (where[longest] + shift) % array.shape[longest]
        spots.append(tuple(where))
    return array.at[spots[0]].set(low).at[spots[1]].set(top_value)


def block_levels(key, shape, shards, low, high):
    level, own = 1.0, jax.random.fold_in(key, 6)
    for dim, blocks in shards:
        heights = jnp.exp(jax.random.uniform(jax.random.fold_in(own, dim), (blocks,), jnp.float32, low / len(shards), high / len(shards)))
        level = level * jnp.repeat(heights, shape[dim] // blocks).reshape([-1 if axis == dim else 1 for axis in range(len(shape))])
    return level


def gaussian(key, shape, deviation, limit, cuts=(), kind=jnp.bfloat16):
    result = deviation * jax.random.normal(key, shape, jnp.float32)
    if cuts:
        result = result * block_levels(key, shape, cuts, -0.22, 0.18)
    return jnp.clip(result, -limit, limit).astype(kind)


def setup_inputs(seed: int = 0) -> dict:
    arg_keys = jax.random.split(jax.random.key(seed), 7)
    trial = gaussian(arg_keys[0], (2, NB, BLK, BLK), 1.0, 6.0, ((1, 32),))
    left_env = gaussian(arg_keys[1], (MB, NL, BLK, BLK), BLK ** -0.5, 0.5, ((0, 8), (1, 32)))
    right_env = gaussian(arg_keys[2], (MB, NR, BLK, BLK), (BLK * MB) ** -0.5, 0.109375, ((0, 8), (1, 32)))
    left_slot = with_ends(jax.random.randint(arg_keys[3], (NB,), 0, NL_DEV), jax.random.fold_in(arg_keys[3], 1), 0, NL_DEV - 1).astype(jnp.int32)
    dest = draw_dest(jax.random.fold_in(arg_keys[6], 71), 0)
    right_slot = with_ends(jax.random.randint(arg_keys[5], (NB,), 0, NR_DEV), jax.random.fold_in(arg_keys[5], 1), 0, NR_DEV - 1).astype(jnp.int32)
    return dict(trial=trial, left_env=left_env, right_env=right_env, left_slot=left_slot, dest=dest, right_slot=right_slot)


def reference(trial, left_env, right_env, left_slot, dest, right_slot):
    block_total = trial.shape[1]
    targets = dest[:, 0].astype(jnp.int32)
    owner_dev = jnp.arange(block_total, dtype=jnp.int32) // NB_DEV
    left_rows = owner_dev * NL_DEV + left_slot.astype(jnp.int32)
    right_rows = targets * NR_DEV + right_slot.astype(jnp.int32)
    grouped = targets.reshape(N_SEC, NB_DEV)
    order_index = jnp.arange(NB_DEV, dtype=jnp.int32)
    earlier_same = (grouped[:, :, None] == grouped[:, None, :]) & (order_index[None, None, :] < order_index[None, :, None])
    ranks = jnp.sum(earlier_same.astype(jnp.int32), axis=2).reshape(block_total)
    out_rows = ((targets * N_SEC + owner_dev) * CAP + ranks).astype(jnp.int32)

    def apply_block(block_index):
        left_blocks = left_env[:, left_rows[block_index]].astype(jnp.float32)
        right_blocks = right_env[:, right_rows[block_index]].astype(jnp.float32)
        vectors = trial[:, block_index].astype(jnp.float32)
        product = jnp.einsum('bij,vjl->bvil', left_blocks, vectors).astype(jnp.bfloat16)
        product = lax.optimization_barrier(product).astype(jnp.float32)
        partial_value = jnp.einsum('bvil,bml->bvim', product, right_blocks)
        partial_value = partial_value.reshape(N_MPO, MB_DEV, 2, BLK, BLK).sum(axis=1).astype(jnp.bfloat16)
        partial_value = lax.optimization_barrier(partial_value).astype(jnp.float32)
        return jnp.sum(partial_value, axis=0).astype(jnp.bfloat16)

    results = lax.map(apply_block, jnp.arange(block_total, dtype=jnp.int32))
    applied = jnp.zeros((RECV, 2, BLK, BLK), jnp.bfloat16).at[out_rows].set(results)
    return applied
```

```python
import jax
import jax.numpy as jnp
from jax import lax
from jax.sharding import PartitionSpec as P


def rank_within(rows):
    width = rows.shape[-1]
    order_index = jnp.arange(width, dtype=jnp.int32)
    earlier_same = (rows[:, :, None] == rows[:, None, :]) & (
        order_index[None, None, :] < order_index[None, :, None]
    )
    return jnp.sum(earlier_same.astype(jnp.int32), axis=2)


def local(trial, left_env, right_env, left_slot, dest, right_slot):
    sec_count = lax.axis_size("sec")
    block_count = trial.shape[1]
    capacity = max(2, 2 * block_count // sec_count)
    slots = sec_count * capacity
    my_sec = lax.axis_index("sec")
    targets = dest[:, 0]
    table = lax.all_gather(jnp.stack([targets, right_slot]), "sec", axis=0, tiled=False)
    target_table, right_table = table[:, 0], table[:, 1]
    table_ranks = rank_within(target_table)
    cap_index = jnp.arange(capacity, dtype=jnp.int32)
    recv_match = (target_table[:, None, :] == my_sec) & (
        table_ranks[:, None, :] == cap_index[None, :, None]
    )
    asked = jnp.sum(jnp.where(recv_match, right_table[:, None, :], 0), axis=2).reshape(slots)
    own_ranks = rank_within(targets[None, :])[0]
    positions = targets * capacity + own_ranks
    slot_match = positions[None, :] == jnp.arange(slots, dtype=jnp.int32)[:, None]
    slot_block = jnp.sum(
        jnp.where(slot_match, jnp.arange(block_count, dtype=jnp.int32)[None, :], 0), axis=1
    )
    slot_live = jnp.any(slot_match, axis=1)
    outgoing = jnp.take(right_env, asked, axis=1)
    incoming = lax.all_to_all(outgoing, "sec", split_axis=1, concat_axis=1, tiled=True)
    left_blocks = jnp.take(left_env, left_slot, axis=1)
    products = jnp.einsum(
        "bkij,vkjl->bvkil", left_blocks, trial, preferred_element_type=jnp.float32
    ).astype(jnp.bfloat16)
    right_blocks = jnp.take(incoming, positions, axis=1)
    partials = jnp.einsum(
        "bvkil,bkml->kvim", products, right_blocks, preferred_element_type=jnp.float32
    ).astype(jnp.bfloat16)
    summed = lax.psum_scatter(partials, "mpo", scatter_dimension=2, tiled=True)
    placed = jnp.where(
        slot_live[:, None, None, None], jnp.take(summed, slot_block, axis=0), 0
    )
    placed = lax.all_to_all(placed, "sec", split_axis=0, concat_axis=0, tiled=True)
    return lax.all_to_all(placed, "mpo", split_axis=0, concat_axis=2, tiled=True)


def solution(mesh):
    placed = (
        P(None, "sec", None, None),
        P("mpo", "sec", None, None),
        P("mpo", "sec", None, None),
        P("sec"),
        P("sec", None),
        P("sec"),
    )
    return jax.shard_map(
        local,
        mesh=mesh,
        in_specs=placed,
        out_specs=P(("sec", "mpo"), None, None, None),
        check_vma=False,
    )
```

```python
import jax
import jax.numpy as jnp
from jax import lax
from jax.experimental import pallas as pl
from jax.experimental.pallas import tpu as pltpu
from jax.sharding import PartitionSpec as P

MESH = pl.DeviceIdType.MESH
CHIPS = (
    (0, 0), (0, 1), (1, 0), (0, 3),
    (3, 0), (1, 1), (3, 3), (1, 3),
    (3, 1), (2, 0), (0, 2), (2, 1),
    (1, 2), (2, 3), (3, 2), (2, 2),
)
WINDOW = 4
CHUNKS = len(CHIPS)
F32 = jnp.float32
BF16 = jnp.bfloat16


def flip(value, bits):
    high, low = value // 2, value % 2
    return ((high + bits // 2) % 2) * 2 + (low + bits % 2) % 2


def kernel(
    trial, left, right, lslot, dest, rslot, out,
    tv, lv, rv, xb, sendb, recvb, part, ring, total, crossed,
    ktab, rtab, itab, ktab_s, itab_s,
    load_sem, tab_sem, isend, irecv, rsend, rrecv, gsend, grecv, csend, crecv, zsend, zrecv,
):
    me = lax.axis_index("sec")
    z = lax.axis_index("mpo")
    core, x, y = me % 2, (me // 2) % 4, me // 8
    depth = 1 - 2 * core
    planes = 8

    def partner(chunk, i):
        dy, dx = CHIPS[chunk]
        return flip(y, dy) * 8 + flip(x, dx) * 2 + (core + i) % 2

    everyone = [(t, i) for t in range(CHUNKS) for i in range(2) if (t, i) != (0, 0)]

    barrier = pltpu.get_barrier_semaphore()
    for t, i in everyone:
        pl.semaphore_signal(
            barrier, inc=1, device_id={"sec": partner(t, i)}, device_id_type=MESH
        )
    for step in range(1, planes):
        pl.semaphore_signal(
            barrier, inc=1, device_id={"mpo": (z + step) % planes}, device_id_type=MESH
        )
    loads = [
        pltpu.make_async_copy(right, rv, load_sem.at[0]),
        pltpu.make_async_copy(trial, tv, load_sem.at[1]),
        pltpu.make_async_copy(left, lv, load_sem.at[2]),
    ]
    for load in loads:
        load.start()

    lane = lax.broadcasted_iota(jnp.int32, (1, 128), 1)
    seen = jnp.zeros((1, 128), jnp.int32)
    first_k = jnp.full((1, 128), -1, jnp.int32)
    second_k = jnp.full((1, 128), -1, jnp.int32)
    first_r = jnp.zeros((1, 128), jnp.int32)
    second_r = jnp.zeros((1, 128), jnp.int32)
    for k in range(24):
        hit = lane == dest[k, 0]
        is_first = hit & (seen == 0)
        is_second = hit & (seen == 1)
        first_k = jnp.where(is_first, k, first_k)
        second_k = jnp.where(is_second, k, second_k)
        first_r = jnp.where(is_first, rslot[k], first_r)
        second_r = jnp.where(is_second, rslot[k], second_r)
        seen = seen + hit.astype(jnp.int32)
    ktab[0:1, :] = first_k
    ktab[1:2, :] = second_k
    rtab[0:1, :] = first_r
    rtab[1:2, :] = second_r
    to_smem = pltpu.make_async_copy(ktab, ktab_s, tab_sem.at[0])
    to_smem.start()
    to_smem.wait()

    pl.semaphore_wait(barrier, len(everyone) + planes - 1)

    asks = []
    for t, i in everyone:
        o = 2 * t + i
        asks.append(
            pltpu.make_async_remote_copy(
                src_ref=rtab, dst_ref=itab.at[o], send_sem=isend.at[o], recv_sem=irecv.at[o],
                device_id={"sec": partner(t, i)}, device_id_type=MESH,
            )
        )
        asks[-1].start()
    itab[0] = rtab[...]
    loads[0].wait()
    for ask in asks:
        ask.wait_recv()
    asked = pltpu.make_async_copy(itab, itab_s, tab_sem.at[1])
    asked.start()
    asked.wait()

    def whole(t, i):
        o = 2 * t + i
        return pltpu.make_async_remote_copy(
            src_ref=sendb.at[o], dst_ref=recvb.at[o], send_sem=rsend.at[o], recv_sem=rrecv.at[o],
            device_id={"sec": partner(t, i)}, device_id_type=MESH,
        )

    def send_window(start):
        group = [(t, i) for t in range(start, start + WINDOW) for i in range(2)]
        for c in range(2):
            for t, i in group:
                o = 2 * t + i
                slot = itab_s[o, c, me]
                for b in range(3):
                    if o == 0:
                        recvb[0, c, b] = rv[b, slot]
                    else:
                        sendb[o, c, b] = rv[b, slot]
            for b in range(3):
                for t, i in group:
                    o = 2 * t + i
                    if o:
                        pltpu.make_async_remote_copy(
                            src_ref=sendb.at[o, c, b], dst_ref=recvb.at[o, c, b],
                            send_sem=rsend.at[o], recv_sem=rrecv.at[o],
                            device_id={"sec": partner(t, i)}, device_id_type=MESH,
                        ).start()

    def left_products():
        def body(k, carry):
            a = lslot[k]
            stacked = jnp.concatenate([lv[b, a] for b in range(3)], axis=0)
            vectors = jnp.concatenate([tv[0, k], tv[1, k]], axis=1)
            product = jnp.dot(stacked, vectors, preferred_element_type=F32).astype(BF16)
            for b in range(3):
                for v in range(2):
                    xb[k, b, v * 128 : (v + 1) * 128, :] = product[
                        b * 128 : (b + 1) * 128, v * 128 : (v + 1) * 128
                    ]
            return carry

        lax.fori_loop(0, 24, body, 0)

    def right_products(t):
        for i in range(2):
            if (t, i) != (0, 0):
                whole(t, i).wait_recv()

        def body(q, carry):
            i, c = q // 2, q % 2
            k = ktab_s[c, partner(t, i)]
            at = jnp.maximum(k, 0)
            o = 2 * t + i
            xs = jnp.concatenate([xb[at, b] for b in range(3)], axis=1)
            rs = jnp.concatenate([recvb[o, c, b] for b in range(3)], axis=1)
            value = lax.dot_general(xs, rs, (((1,), (1,)), ((), ())), preferred_element_type=F32)
            value = jnp.where(k >= 0, value, 0.0).astype(BF16)
            for v in range(2):
                for p in range(planes):
                    row = v * 128 + p * 16
                    part[t, p, q * 2 + v] = value[row : row + 16]
            return carry

        lax.fori_loop(0, 4, body, 0)

    def hop(t, slot):
        if slot < 4:
            piece = (z + planes + (slot - 4) * depth) % planes
            to = (z + planes - depth) % planes
        else:
            piece = (z + planes + (7 - slot) * depth) % planes
            to = (z + planes + depth) % planes
        return pltpu.make_async_remote_copy(
            src_ref=part.at[t, piece], dst_ref=ring.at[t, slot],
            send_sem=gsend.at[t, slot], recv_sem=grecv.at[t, slot],
            device_id={"mpo": to}, device_id_type=MESH,
        )

    def add_in(t, slot):
        hop(t, slot - 1).wait_recv()
        if slot < 4:
            piece = (z + planes + (slot - 4) * depth) % planes
        else:
            piece = (z + planes + (7 - slot) * depth) % planes
        part[t, piece] = (part[t, piece].astype(F32) + ring[t, slot - 1].astype(F32)).astype(BF16)

    def ring_step(t, step):
        if step:
            add_in(t, step)
        hop(t, step).start()
        if step < 3:
            if step:
                add_in(t, 4 + step)
            hop(t, 4 + step).start()

    def across(t, i):
        o = 2 * t + i
        return pltpu.make_async_remote_copy(
            src_ref=total.at[t, pl.ds(4 * i, 4)], dst_ref=crossed.at[o],
            send_sem=csend.at[o], recv_sem=crecv.at[o],
            device_id={"sec": partner(t, i)}, device_id_type=MESH,
        )

    def finish_sum(t):
        hop(t, 3).wait_recv()
        hop(t, 6).wait_recv()
        done = (
            part[t, z].astype(F32) + ring[t, 3].astype(F32) + ring[t, 6].astype(F32)
        ).astype(BF16)
        total[t] = done
        for i in range(2):
            if (t, i) == (0, 0):
                crossed[0] = done[0:4]
            else:
                across(t, i).start()

    def place(t, i):
        source = partner(t, i)
        to, w = source // 4, source % 4
        src = crossed.at[2 * t + i]
        return to, pltpu.make_async_remote_copy(
            src_ref=src, dst_ref=out.at[pl.ds(4 * w, 4), pl.ds(16 * z, 16)],
            send_sem=zsend.at[2 * t + i], recv_sem=zrecv.at[w, z],
            device_id={"mpo": to}, device_id_type=MESH,
        ), pltpu.make_async_copy(
            src, out.at[pl.ds(4 * w, 4), pl.ds(16 * z, 16)], zrecv.at[w, z]
        )

    def place_rows(t):
        for i in range(2):
            if (t, i) != (0, 0):
                across(t, i).wait_recv()
            to, remote, own = place(t, i)

            @pl.when(to == z)
            def _():
                own.start()

            @pl.when(to != z)
            def _():
                remote.start()

    send_window(0)
    send_window(WINDOW)
    loads[1].wait()
    loads[2].wait()
    left_products()
    for turn in range(CHUNKS + 5):
        if 0 <= turn - 5 < CHUNKS:
            place_rows(turn - 5)
        if 0 <= turn - 4 < CHUNKS:
            finish_sum(turn - 4)
        for step in (3, 2, 1):
            if 0 <= turn - step < CHUNKS:
                ring_step(turn - step, step)
        if turn < CHUNKS:
            if turn % WINDOW == 0 and turn + 2 * WINDOW < CHUNKS:
                send_window(turn + 2 * WINDOW)
            right_products(turn)
            ring_step(turn, 0)

    for ask in asks:
        ask.wait_send()
    for t, i in everyone:
        whole(t, i).wait_send()
        across(t, i).wait_send()
    for t in range(CHUNKS):
        for slot in range(7):
            hop(t, slot).wait_send()
        for i in range(2):
            to, remote, own = place(t, i)

            @pl.when(to != z)
            def _():
                remote.wait_send()
    for w in range(4):
        for p in range(planes):
            pltpu.make_async_copy(
                crossed.at[0], out.at[pl.ds(4 * w, 4), pl.ds(16 * p, 16)], zrecv.at[w, p]
            ).wait()


def local(trial, left_env, right_env, left_slot, dest, right_slot):
    anywhere = pl.BlockSpec(memory_space=pl.ANY)
    scalars = pl.BlockSpec(memory_space=pltpu.SMEM)
    dma = pltpu.SemaphoreType.DMA
    rows = pl.pallas_call(
        kernel,
        out_shape=jax.ShapeDtypeStruct((16, 128, 128), BF16),
        in_specs=[anywhere] * 3 + [scalars] * 3,
        out_specs=anywhere,
        scratch_shapes=[
            pltpu.VMEM((2, 24, 128, 128), BF16),
            pltpu.VMEM((3, 32, 128, 128), BF16),
            pltpu.VMEM((3, 32, 128, 128), BF16),
            pltpu.VMEM((24, 3, 256, 128), BF16),
            pltpu.VMEM((32, 2, 3, 128, 128), BF16),
            pltpu.VMEM((32, 2, 3, 128, 128), BF16),
            pltpu.VMEM((CHUNKS, 8, 8, 16, 128), BF16),
            pltpu.VMEM((CHUNKS, 7, 8, 16, 128), BF16),
            pltpu.VMEM((CHUNKS, 8, 16, 128), BF16),
            pltpu.VMEM((32, 4, 16, 128), BF16),
            pltpu.VMEM((2, 128), jnp.int32),
            pltpu.VMEM((2, 128), jnp.int32),
            pltpu.VMEM((32, 2, 128), jnp.int32),
            pltpu.SMEM((2, 128), jnp.int32),
            pltpu.SMEM((32, 2, 128), jnp.int32),
            dma((3,)),
            dma((2,)),
            dma((32,)),
            dma((32,)),
            dma((32,)),
            dma((32,)),
            dma((CHUNKS, 7)),
            dma((CHUNKS, 7)),
            dma((32,)),
            dma((32,)),
            dma((32,)),
            dma((4, 8)),
        ],
        compiler_params=pltpu.CompilerParams(
            collective_id=0, has_side_effects=True, vmem_limit_bytes=50 * 1024 * 1024
        ),
        name="products",
    )(trial, left_env, right_env, left_slot, dest, right_slot)
    return rows.reshape(8, 2, 128, 128)


def solution(mesh):
    placed = (
        P(None, "sec", None, None),
        P("mpo", "sec", None, None),
        P("mpo", "sec", None, None),
        P("sec"),
        P("sec", None),
        P("sec"),
    )
    return jax.shard_map(
        local,
        mesh=mesh,
        in_specs=placed,
        out_specs=P(("sec", "mpo"), None, None, None),
        check_vma=False,
    )
```

```python
import jax
import jax.numpy as jnp
from jax import lax
from jax.experimental import pallas as pl
from jax.experimental.pallas import tpu as pltpu
from jax.sharding import PartitionSpec as P

MESH = pl.DeviceIdType.MESH
CHIPS = (
    (0, 0), (0, 1), (1, 0), (0, 3),
    (3, 0), (1, 1), (3, 3), (1, 3),
    (3, 1), (2, 0), (0, 2), (2, 1),
    (1, 2), (2, 3), (3, 2), (2, 2),
)
AHEAD = 6
SLACK = 3
CHUNKS = len(CHIPS)
F32 = jnp.float32
BF16 = jnp.bfloat16


def flip(value, bits):
    high, low = value // 2, value % 2
    return ((high + bits // 2) % 2) * 2 + (low + bits % 2) % 2


def kernel(
    trial, left, right, lslot_hbm, dest_hbm, rslot_hbm, out,
    tv, lv, rv, xb, sendb, recvb, part, ring, total, crossed,
    ktab, rtab, itab, ktab_s, itab_s, lslot, dest, rslot,
    load_sem, small_sem, tab_sem, isend, irecv, rsend, rrecv, gsend, grecv, csend, crecv, zsend, zrecv,
):
    me = lax.axis_index("sec")
    z = lax.axis_index("mpo")
    core, x, y = me % 2, (me // 2) % 4, me // 8
    depth = 1 - 2 * core
    planes = 8

    def partner(chunk, i):
        dy, dx = CHIPS[chunk]
        return flip(y, dy) * 8 + flip(x, dx) * 2 + (core + i) % 2

    everyone = [(t, i) for t in range(CHUNKS) for i in range(2) if (t, i) != (0, 0)]

    smalls = [
        pltpu.make_async_copy(dest_hbm, dest, small_sem.at[0]),
        pltpu.make_async_copy(rslot_hbm, rslot, small_sem.at[1]),
        pltpu.make_async_copy(lslot_hbm, lslot, small_sem.at[2]),
    ]
    for small in smalls:
        small.start()

    barrier = pltpu.get_barrier_semaphore()
    for t, i in everyone:
        pl.semaphore_signal(
            barrier, inc=1, device_id={"sec": partner(t, i)}, device_id_type=MESH
        )
    for step in range(1, planes):
        pl.semaphore_signal(
            barrier, inc=1, device_id={"mpo": (z + step) % planes}, device_id_type=MESH
        )
    loads = [
        pltpu.make_async_copy(right, rv, load_sem.at[0]),
        pltpu.make_async_copy(trial, tv, load_sem.at[1]),
        pltpu.make_async_copy(left, lv, load_sem.at[2]),
    ]
    for load in loads:
        load.start()

    for small in smalls:
        small.wait()

    lane = lax.broadcasted_iota(jnp.int32, (1, 128), 1)
    seen = jnp.zeros((1, 128), jnp.int32)
    first_k = jnp.full((1, 128), -1, jnp.int32)
    second_k = jnp.full((1, 128), -1, jnp.int32)
    first_r = jnp.zeros((1, 128), jnp.int32)
    second_r = jnp.zeros((1, 128), jnp.int32)
    for k in range(24):
        hit = lane == dest[k, 0]
        is_first = hit & (seen == 0)
        is_second = hit & (seen == 1)
        first_k = jnp.where(is_first, k, first_k)
        second_k = jnp.where(is_second, k, second_k)
        first_r = jnp.where(is_first, rslot[k], first_r)
        second_r = jnp.where(is_second, rslot[k], second_r)
        seen = seen + hit.astype(jnp.int32)
    ktab[0:1, :] = first_k
    ktab[1:2, :] = second_k
    rtab[0:1, :] = first_r
    rtab[1:2, :] = second_r
    to_smem = pltpu.make_async_copy(ktab, ktab_s, tab_sem.at[0])
    to_smem.start()
    to_smem.wait()

    pl.semaphore_wait(barrier, len(everyone) + planes - 1)

    for t, i in everyone:
        o = 2 * t + i
        pltpu.make_async_remote_copy(
            src_ref=rtab, dst_ref=itab.at[o], send_sem=isend, recv_sem=irecv,
            device_id={"sec": partner(t, i)}, device_id_type=MESH,
        ).start()
    itab[0] = rtab[...]
    loads[0].wait()
    all_asks = pltpu.make_async_copy(itab.at[pl.ds(1, 31)], itab.at[pl.ds(1, 31)], irecv)
    all_asks.wait()
    asked = pltpu.make_async_copy(itab, itab_s, tab_sem.at[1])
    asked.start()
    asked.wait()

    def send_chunk(t):
        for c in range(2):
            for i in range(2):
                o = 2 * t + i
                slot = itab_s[o, c, me]
                for b in range(3):
                    if o == 0:
                        recvb[0, c, b] = rv[b, slot]
                    else:
                        sendb[o, c, b] = rv[b, slot]
            for b in range(3):
                for i in range(2):
                    o = 2 * t + i
                    if o:
                        pltpu.make_async_remote_copy(
                            src_ref=sendb.at[o, c, b], dst_ref=recvb.at[o, c, b],
                            send_sem=rsend, recv_sem=rrecv.at[t],
                            device_id={"sec": partner(t, i)}, device_id_type=MESH,
                        ).start()

    def left_products():
        def body(k, carry):
            a = lslot[k]
            stacked = jnp.concatenate([lv[b, a] for b in range(3)], axis=0)
            vectors = jnp.concatenate([tv[0, k], tv[1, k]], axis=1)
            product = jnp.dot(stacked, vectors, preferred_element_type=F32).astype(BF16)
            for b in range(3):
                for v in range(2):
                    xb[k, b, v * 128 : (v + 1) * 128, :] = product[
                        b * 128 : (b + 1) * 128, v * 128 : (v + 1) * 128
                    ]
            return carry

        lax.fori_loop(0, 24, body, 0)

    def right_products(t):
        landed = recvb.at[pl.ds(2 * t, 2)] if t else recvb.at[1]
        pltpu.make_async_copy(landed, landed, rrecv.at[t]).wait()

        def body(q, carry):
            i, c = q // 2, q % 2
            k = ktab_s[c, partner(t, i)]
            at = jnp.maximum(k, 0)
            o = 2 * t + i
            xs = jnp.concatenate([xb[at, b] for b in range(3)], axis=1)
            rs = jnp.concatenate([recvb[o, c, b] for b in range(3)], axis=1)
            value = lax.dot_general(xs, rs, (((1,), (1,)), ((), ())), preferred_element_type=F32)
            value = jnp.where(k >= 0, value, 0.0).astype(BF16)
            for v in range(2):
                for p in range(planes):
                    row = v * 128 + p * 16
                    part[t, p, q * 2 + v] = value[row : row + 16]
            return carry

        lax.fori_loop(0, 4, body, 0)

    def hop(t, step, way):
        back = 4 - step if way == 0 else step - 3
        piece = (z + planes - back * depth) % planes
        to = (z + planes + (depth if way else -depth)) % planes
        return piece, pltpu.make_async_remote_copy(
            src_ref=part.at[t, piece], dst_ref=ring.at[t, step, way],
            send_sem=gsend, recv_sem=grecv.at[t, step],
            device_id={"mpo": to}, device_id_type=MESH,
        )

    def ring_step(t, step):
        ways = range(2 if step < 3 else 1)
        if step:
            landed = ring.at[t, step - 1]
            pltpu.make_async_copy(landed, landed, grecv.at[t, step - 1]).wait()
        for way in ways:
            piece, copy = hop(t, step, way)
            if step:
                part[t, piece] = (
                    part[t, piece].astype(F32) + ring[t, step - 1, way].astype(F32)
                ).astype(BF16)
            copy.start()

    def across(t, i):
        o = 2 * t + i
        return pltpu.make_async_remote_copy(
            src_ref=total.at[t, pl.ds(4 * i, 4)], dst_ref=crossed.at[o],
            send_sem=csend, recv_sem=crecv.at[t],
            device_id={"sec": partner(t, i)}, device_id_type=MESH,
        )

    def finish_sum(t):
        pltpu.make_async_copy(ring.at[t, 3, 0], ring.at[t, 3, 0], grecv.at[t, 3]).wait()
        done = (
            part[t, z].astype(F32) + ring[t, 3, 0].astype(F32) + ring[t, 2, 1].astype(F32)
        ).astype(BF16)
        total[t] = done
        for i in range(2):
            if (t, i) == (0, 0):
                crossed[0] = done[0:4]
            else:
                across(t, i).start()

    def place(t, i):
        source = partner(t, i)
        to, w = source // 4, source % 4
        src = crossed.at[2 * t + i]
        return to, pltpu.make_async_remote_copy(
            src_ref=src, dst_ref=out.at[pl.ds(4 * w, 4), pl.ds(16 * z, 16)],
            send_sem=zsend, recv_sem=zrecv,
            device_id={"mpo": to}, device_id_type=MESH,
        ), pltpu.make_async_copy(
            src, out.at[pl.ds(4 * w, 4), pl.ds(16 * z, 16)], zrecv
        )

    def place_rows(t):
        landed = crossed.at[pl.ds(2 * t, 2)] if t else crossed.at[1]
        pltpu.make_async_copy(landed, landed, crecv.at[t]).wait()
        for i in range(2):
            to, remote, own = place(t, i)

            @pl.when(to == z)
            def _():
                own.start()

            @pl.when(to != z)
            def _():
                remote.start()

    for t in range(AHEAD):
        send_chunk(t)
    loads[1].wait()
    loads[2].wait()
    left_products()
    for turn in range(CHUNKS + 5 * SLACK):
        if 0 <= turn - 5 * SLACK < CHUNKS:
            place_rows(turn - 5 * SLACK)
        if 0 <= turn - 4 * SLACK < CHUNKS:
            finish_sum(turn - 4 * SLACK)
        for step in (3, 2, 1):
            if 0 <= turn - step * SLACK < CHUNKS:
                ring_step(turn - step * SLACK, step)
        if turn < CHUNKS:
            if turn + AHEAD < CHUNKS:
                send_chunk(turn + AHEAD)
            right_products(turn)
            ring_step(turn, 0)

    for sent, sem in (
        (itab.at[pl.ds(1, 31)], isend),
        (sendb.at[pl.ds(1, 31)], rsend),
        (part.at[:, pl.ds(0, 7)], gsend),
        (crossed.at[pl.ds(1, 31)], csend),
        (crossed.at[pl.ds(0, 28)], zsend),
        (out, zrecv),
    ):
        pltpu.make_async_copy(sent, sent, sem).wait()


def local(trial, left_env, right_env, left_slot, dest, right_slot):
    anywhere = pl.BlockSpec(memory_space=pl.ANY)
    dma = pltpu.SemaphoreType.DMA
    rows = pl.pallas_call(
        kernel,
        out_shape=jax.ShapeDtypeStruct((16, 128, 128), BF16),
        in_specs=[anywhere] * 6,
        out_specs=anywhere,
        scratch_shapes=[
            pltpu.VMEM((2, 24, 128, 128), BF16),
            pltpu.VMEM((3, 32, 128, 128), BF16),
            pltpu.VMEM((3, 32, 128, 128), BF16),
            pltpu.VMEM((24, 3, 256, 128), BF16),
            pltpu.VMEM((32, 2, 3, 128, 128), BF16),
            pltpu.VMEM((32, 2, 3, 128, 128), BF16),
            pltpu.VMEM((CHUNKS, 8, 8, 16, 128), BF16),
            pltpu.VMEM((CHUNKS, 4, 2, 8, 16, 128), BF16),
            pltpu.VMEM((CHUNKS, 8, 16, 128), BF16),
            pltpu.VMEM((32, 4, 16, 128), BF16),
            pltpu.VMEM((2, 128), jnp.int32),
            pltpu.VMEM((2, 128), jnp.int32),
            pltpu.VMEM((32, 2, 128), jnp.int32),
            pltpu.SMEM((2, 128), jnp.int32),
            pltpu.SMEM((32, 2, 128), jnp.int32),
            pltpu.SMEM((24,), jnp.int32),
            pltpu.SMEM((24, 1), jnp.int32),
            pltpu.SMEM((24,), jnp.int32),
            dma((3,)),
            dma((3,)),
            dma((2,)),
            dma,
            dma,
            dma,
            dma((CHUNKS,)),
            dma,
            dma((CHUNKS, 4)),
            dma,
            dma((CHUNKS,)),
            dma,
            dma,
        ],
        compiler_params=pltpu.CompilerParams(
            collective_id=0, has_side_effects=True, vmem_limit_bytes=60 * 1024 * 1024
        ),
        name="products",
    )(trial, left_env, right_env, left_slot, dest, right_slot)
    return rows.reshape(8, 2, 128, 128)


def solution(mesh):
    placed = (
        P(None, "sec", None, None),
        P("mpo", "sec", None, None),
        P("mpo", "sec", None, None),
        P("sec"),
        P("sec", None),
        P("sec"),
    )
    return jax.shard_map(
        local,
        mesh=mesh,
        in_specs=placed,
        out_specs=P(("sec", "mpo"), None, None, None),
        check_vma=False,
    )
```

```python
import jax
import jax.numpy as jnp
from jax import lax
from jax.experimental import pallas as pl
from jax.experimental.pallas import tpu as pltpu
from jax.sharding import PartitionSpec as P

MESH = pl.DeviceIdType.MESH
CHIPS = (
    (0, 0), (0, 1), (1, 0), (0, 3),
    (3, 0), (1, 1), (3, 3), (1, 3),
    (3, 1), (2, 0), (0, 2), (2, 1),
    (1, 2), (2, 3), (3, 2), (2, 2),
)
AHEAD = 6
LAGS = (0, 2, 4, 6, 8, 12)
CHUNKS = len(CHIPS)
F32 = jnp.float32
BF16 = jnp.bfloat16


def flip(value, bits):
    high, low = value // 2, value % 2
    return ((high + bits // 2) % 2) * 2 + (low + bits % 2) % 2


def kernel(
    trial, left, right, lslot_hbm, dest_hbm, rslot_hbm, out,
    tv, lv, rv, xb, sendb, recvb, part, ring, total, crossed,
    ktab, rtab, itab, ktab_s, itab_s, lslot, dest, rslot,
    load_sem, small_sem, tab_sem, isend, irecv, rsend, rrecv, gsend, grecv, csend, crecv, zsend, zrecv,
):
    me = lax.axis_index("sec")
    z = lax.axis_index("mpo")
    core, x, y = me % 2, (me // 2) % 4, me // 8
    depth = 1 - 2 * core
    planes = 8

    def partner(chunk, i):
        dy, dx = CHIPS[chunk]
        return flip(y, dy) * 8 + flip(x, dx) * 2 + (core + i) % 2

    everyone = [(t, i) for t in range(CHUNKS) for i in range(2) if (t, i) != (0, 0)]

    smalls = [
        pltpu.make_async_copy(dest_hbm, dest, small_sem.at[0]),
        pltpu.make_async_copy(rslot_hbm, rslot, small_sem.at[1]),
        pltpu.make_async_copy(lslot_hbm, lslot, small_sem.at[2]),
    ]
    for small in smalls:
        small.start()

    barrier = pltpu.get_barrier_semaphore()
    for t, i in everyone:
        pl.semaphore_signal(
            barrier, inc=1, device_id={"sec": partner(t, i)}, device_id_type=MESH
        )
    for step in range(1, planes):
        pl.semaphore_signal(
            barrier, inc=1, device_id={"mpo": (z + step) % planes}, device_id_type=MESH
        )
    loads = [
        pltpu.make_async_copy(right, rv, load_sem.at[0]),
        pltpu.make_async_copy(trial, tv, load_sem.at[1]),
        pltpu.make_async_copy(left, lv, load_sem.at[2]),
    ]
    for load in loads:
        load.start()

    for small in smalls:
        small.wait()

    lane = lax.broadcasted_iota(jnp.int32, (1, 128), 1)
    seen = jnp.zeros((1, 128), jnp.int32)
    first_k = jnp.full((1, 128), -1, jnp.int32)
    second_k = jnp.full((1, 128), -1, jnp.int32)
    first_r = jnp.zeros((1, 128), jnp.int32)
    second_r = jnp.zeros((1, 128), jnp.int32)
    for k in range(24):
        hit = lane == dest[k, 0]
        is_first = hit & (seen == 0)
        is_second = hit & (seen == 1)
        first_k = jnp.where(is_first, k, first_k)
        second_k = jnp.where(is_second, k, second_k)
        first_r = jnp.where(is_first, rslot[k], first_r)
        second_r = jnp.where(is_second, rslot[k], second_r)
        seen = seen + hit.astype(jnp.int32)
    ktab[0:1, :] = first_k
    ktab[1:2, :] = second_k
    rtab[0:1, :] = first_r
    rtab[1:2, :] = second_r
    to_smem = pltpu.make_async_copy(ktab, ktab_s, tab_sem.at[0])
    to_smem.start()
    to_smem.wait()

    pl.semaphore_wait(barrier, len(everyone) + planes - 1)

    for t, i in everyone:
        o = 2 * t + i
        pltpu.make_async_remote_copy(
            src_ref=rtab, dst_ref=itab.at[o], send_sem=isend, recv_sem=irecv,
            device_id={"sec": partner(t, i)}, device_id_type=MESH,
        ).start()
    itab[0] = rtab[...]
    loads[0].wait()
    all_asks = pltpu.make_async_copy(itab.at[pl.ds(1, 31)], itab.at[pl.ds(1, 31)], irecv)
    all_asks.wait()
    asked = pltpu.make_async_copy(itab, itab_s, tab_sem.at[1])
    asked.start()
    asked.wait()

    def send_chunk(t):
        for c in range(2):
            for i in range(2):
                o = 2 * t + i
                slot = itab_s[o, c, me]
                for b in range(3):
                    if o == 0:
                        recvb[0, c, b] = rv[b, slot]
                    else:
                        sendb[o, c, b] = rv[b, slot]
            for b in range(3):
                for i in range(2):
                    o = 2 * t + i
                    if o:
                        pltpu.make_async_remote_copy(
                            src_ref=sendb.at[o, c, b], dst_ref=recvb.at[o, c, b],
                            send_sem=rsend, recv_sem=rrecv.at[t],
                            device_id={"sec": partner(t, i)}, device_id_type=MESH,
                        ).start()

    def left_products():
        def body(k, carry):
            a = lslot[k]
            stacked = jnp.concatenate([lv[b, a] for b in range(3)], axis=0)
            vectors = jnp.concatenate([tv[0, k], tv[1, k]], axis=1)
            product = jnp.dot(stacked, vectors, preferred_element_type=F32).astype(BF16)
            for b in range(3):
                for v in range(2):
                    xb[k, b, v * 128 : (v + 1) * 128, :] = product[
                        b * 128 : (b + 1) * 128, v * 128 : (v + 1) * 128
                    ]
            return carry

        lax.fori_loop(0, 24, body, 0)

    def right_products(t):
        landed = recvb.at[pl.ds(2 * t, 2)] if t else recvb.at[1]
        pltpu.make_async_copy(landed, landed, rrecv.at[t]).wait()

        def body(q, carry):
            i, c = q // 2, q % 2
            k = ktab_s[c, partner(t, i)]
            at = jnp.maximum(k, 0)
            o = 2 * t + i
            xs = jnp.concatenate([xb[at, b] for b in range(3)], axis=1)
            rs = jnp.concatenate([recvb[o, c, b] for b in range(3)], axis=1)
            value = lax.dot_general(xs, rs, (((1,), (1,)), ((), ())), preferred_element_type=F32)
            value = jnp.where(k >= 0, value, 0.0).astype(BF16)
            for v in range(2):
                for p in range(planes):
                    row = v * 128 + p * 16
                    part[t, p, q * 2 + v] = value[row : row + 16]
            return carry

        lax.fori_loop(0, 4, body, 0)

    def hop(t, step, way):
        back = 4 - step if way == 0 else step - 3
        piece = (z + planes - back * depth) % planes
        to = (z + planes + (depth if way else -depth)) % planes
        return piece, pltpu.make_async_remote_copy(
            src_ref=part.at[t, piece], dst_ref=ring.at[t, step, way],
            send_sem=gsend, recv_sem=grecv.at[t, step],
            device_id={"mpo": to}, device_id_type=MESH,
        )

    def ring_step(t, step):
        ways = range(2 if step < 3 else 1)
        if step:
            landed = ring.at[t, step - 1]
            pltpu.make_async_copy(landed, landed, grecv.at[t, step - 1]).wait()
        for way in ways:
            piece, copy = hop(t, step, way)
            if step:
                part[t, piece] = (
                    part[t, piece].astype(F32) + ring[t, step - 1, way].astype(F32)
                ).astype(BF16)
            copy.start()

    def across(t, i):
        o = 2 * t + i
        return pltpu.make_async_remote_copy(
            src_ref=total.at[t, pl.ds(4 * i, 4)], dst_ref=crossed.at[o],
            send_sem=csend, recv_sem=crecv.at[t],
            device_id={"sec": partner(t, i)}, device_id_type=MESH,
        )

    def finish_sum(t):
        pltpu.make_async_copy(ring.at[t, 3, 0], ring.at[t, 3, 0], grecv.at[t, 3]).wait()
        done = (
            part[t, z].astype(F32) + ring[t, 3, 0].astype(F32) + ring[t, 2, 1].astype(F32)
        ).astype(BF16)
        total[t] = done
        for i in range(2):
            if (t, i) == (0, 0):
                crossed[0] = done[0:4]
            else:
                across(t, i).start()

    def place(t, i):
        source = partner(t, i)
        to, w = source // 4, source % 4
        src = crossed.at[2 * t + i]
        return to, pltpu.make_async_remote_copy(
            src_ref=src, dst_ref=out.at[pl.ds(4 * w, 4), pl.ds(16 * z, 16)],
            send_sem=zsend, recv_sem=zrecv,
            device_id={"mpo": to}, device_id_type=MESH,
        ), pltpu.make_async_copy(
            src, out.at[pl.ds(4 * w, 4), pl.ds(16 * z, 16)], zrecv
        )

    def place_rows(t):
        landed = crossed.at[pl.ds(2 * t, 2)] if t else crossed.at[1]
        pltpu.make_async_copy(landed, landed, crecv.at[t]).wait()
        for i in range(2):
            to, remote, own = place(t, i)

            @pl.when(to == z)
            def _():
                own.start()

            @pl.when(to != z)
            def _():
                remote.start()

    for t in range(AHEAD):
        send_chunk(t)
    loads[1].wait()
    loads[2].wait()
    left_products()
    for turn in range(CHUNKS + LAGS[5]):
        if 0 <= turn - LAGS[5] < CHUNKS:
            place_rows(turn - LAGS[5])
        if 0 <= turn - LAGS[4] < CHUNKS:
            finish_sum(turn - LAGS[4])
        for step in (3, 2, 1):
            if 0 <= turn - LAGS[step] < CHUNKS:
                ring_step(turn - LAGS[step], step)
        if turn < CHUNKS:
            if turn + AHEAD < CHUNKS:
                send_chunk(turn + AHEAD)
            right_products(turn)
            ring_step(turn, 0)

    for sent, sem in (
        (itab.at[pl.ds(1, 31)], isend),
        (sendb.at[pl.ds(1, 31)], rsend),
        (part.at[:, pl.ds(0, 7)], gsend),
        (crossed.at[pl.ds(1, 31)], csend),
        (crossed.at[pl.ds(0, 28)], zsend),
        (out, zrecv),
    ):
        pltpu.make_async_copy(sent, sent, sem).wait()


def local(trial, left_env, right_env, left_slot, dest, right_slot):
    anywhere = pl.BlockSpec(memory_space=pl.ANY)
    dma = pltpu.SemaphoreType.DMA
    rows = pl.pallas_call(
        kernel,
        out_shape=jax.ShapeDtypeStruct((16, 128, 128), BF16),
        in_specs=[anywhere] * 6,
        out_specs=anywhere,
        scratch_shapes=[
            pltpu.VMEM((2, 24, 128, 128), BF16),
            pltpu.VMEM((3, 32, 128, 128), BF16),
            pltpu.VMEM((3, 32, 128, 128), BF16),
            pltpu.VMEM((24, 3, 256, 128), BF16),
            pltpu.VMEM((32, 2, 3, 128, 128), BF16),
            pltpu.VMEM((32, 2, 3, 128, 128), BF16),
            pltpu.VMEM((CHUNKS, 8, 8, 16, 128), BF16),
            pltpu.VMEM((CHUNKS, 4, 2, 8, 16, 128), BF16),
            pltpu.VMEM((CHUNKS, 8, 16, 128), BF16),
            pltpu.VMEM((32, 4, 16, 128), BF16),
            pltpu.VMEM((2, 128), jnp.int32),
            pltpu.VMEM((2, 128), jnp.int32),
            pltpu.VMEM((32, 2, 128), jnp.int32),
            pltpu.SMEM((2, 128), jnp.int32),
            pltpu.SMEM((32, 2, 128), jnp.int32),
            pltpu.SMEM((24,), jnp.int32),
            pltpu.SMEM((24, 1), jnp.int32),
            pltpu.SMEM((24,), jnp.int32),
            dma((3,)),
            dma((3,)),
            dma((2,)),
            dma,
            dma,
            dma,
            dma((CHUNKS,)),
            dma,
            dma((CHUNKS, 4)),
            dma,
            dma((CHUNKS,)),
            dma,
            dma,
        ],
        compiler_params=pltpu.CompilerParams(
            collective_id=0, has_side_effects=True, vmem_limit_bytes=60 * 1024 * 1024
        ),
        name="products",
    )(trial, left_env, right_env, left_slot, dest, right_slot)
    return rows.reshape(8, 2, 128, 128)


def solution(mesh):
    placed = (
        P(None, "sec", None, None),
        P("mpo", "sec", None, None),
        P("mpo", "sec", None, None),
        P("sec"),
        P("sec", None),
        P("sec"),
    )
    return jax.shard_map(
        local,
        mesh=mesh,
        in_specs=placed,
        out_specs=P(("sec", "mpo"), None, None, None),
        check_vma=False,
    )
```

```python
import jax
import jax.numpy as jnp
from jax import lax
from jax.experimental import pallas as pl
from jax.experimental.pallas import tpu as pltpu
from jax.sharding import PartitionSpec as P

MESH = pl.DeviceIdType.MESH
CHIPS = (
    (0, 0), (0, 1), (1, 0), (0, 3),
    (3, 0), (1, 1), (3, 3), (1, 3),
    (3, 1), (2, 0), (0, 2), (2, 1),
    (1, 2), (2, 3), (3, 2), (2, 2),
)
AHEAD = 6
LAGS = (0, 2, 4, 6, 8, 13)
CHUNKS = len(CHIPS)
F32 = jnp.float32
BF16 = jnp.bfloat16


def flip(value, bits):
    high, low = value // 2, value % 2
    return ((high + bits // 2) % 2) * 2 + (low + bits % 2) % 2


def kernel(
    trial, left, right, lslot_hbm, dest_hbm, rslot_hbm, out,
    tv, lv, rv, xb, sendb, recvb, part, ring, total, crossed,
    ktab, rtab, itab, ktab_s, itab_s, lslot, dest, rslot,
    load_sem, small_sem, tab_sem, isend, irecv, rsend, rrecv, gsend, grecv, csend, crecv, zsend, zrecv,
):
    me = lax.axis_index("sec")
    z = lax.axis_index("mpo")
    core, x, y = me % 2, (me // 2) % 4, me // 8
    depth = 1 - 2 * core
    planes = 8

    def partner(chunk, i):
        dy, dx = CHIPS[chunk]
        return flip(y, dy) * 8 + flip(x, dx) * 2 + (core + i) % 2

    everyone = [(t, i) for t in range(CHUNKS) for i in range(2) if (t, i) != (0, 0)]

    smalls = [
        pltpu.make_async_copy(dest_hbm, dest, small_sem.at[0]),
        pltpu.make_async_copy(rslot_hbm, rslot, small_sem.at[1]),
        pltpu.make_async_copy(lslot_hbm, lslot, small_sem.at[2]),
    ]
    for small in smalls:
        small.start()

    barrier = pltpu.get_barrier_semaphore()
    for t, i in everyone:
        pl.semaphore_signal(
            barrier, inc=1, device_id={"sec": partner(t, i)}, device_id_type=MESH
        )
    for step in range(1, planes):
        pl.semaphore_signal(
            barrier, inc=1, device_id={"mpo": (z + step) % planes}, device_id_type=MESH
        )
    loads = [
        pltpu.make_async_copy(right, rv, load_sem.at[0]),
        pltpu.make_async_copy(trial, tv, load_sem.at[1]),
        pltpu.make_async_copy(left, lv, load_sem.at[2]),
    ]
    for load in loads:
        load.start()

    for small in smalls:
        small.wait()

    lane = lax.broadcasted_iota(jnp.int32, (1, 128), 1)
    seen = jnp.zeros((1, 128), jnp.int32)
    first_k = jnp.full((1, 128), -1, jnp.int32)
    second_k = jnp.full((1, 128), -1, jnp.int32)
    first_r = jnp.zeros((1, 128), jnp.int32)
    second_r = jnp.zeros((1, 128), jnp.int32)
    for k in range(24):
        hit = lane == dest[k, 0]
        is_first = hit & (seen == 0)
        is_second = hit & (seen == 1)
        first_k = jnp.where(is_first, k, first_k)
        second_k = jnp.where(is_second, k, second_k)
        first_r = jnp.where(is_first, rslot[k], first_r)
        second_r = jnp.where(is_second, rslot[k], second_r)
        seen = seen + hit.astype(jnp.int32)
    ktab[0:1, :] = first_k
    ktab[1:2, :] = second_k
    rtab[0:1, :] = first_r
    rtab[1:2, :] = second_r
    to_smem = pltpu.make_async_copy(ktab, ktab_s, tab_sem.at[0])
    to_smem.start()
    to_smem.wait()

    pl.semaphore_wait(barrier, len(everyone) + planes - 1)

    for t, i in everyone:
        o = 2 * t + i
        pltpu.make_async_remote_copy(
            src_ref=rtab, dst_ref=itab.at[o], send_sem=isend, recv_sem=irecv,
            device_id={"sec": partner(t, i)}, device_id_type=MESH,
        ).start()
    itab[0] = rtab[...]
    loads[0].wait()
    all_asks = pltpu.make_async_copy(itab.at[pl.ds(1, 31)], itab.at[pl.ds(1, 31)], irecv)
    all_asks.wait()
    asked = pltpu.make_async_copy(itab, itab_s, tab_sem.at[1])
    asked.start()
    asked.wait()

    def send_chunk(t):
        for c in range(2):
            for i in range(2):
                o = 2 * t + i
                slot = itab_s[o, c, me]
                for b in range(3):
                    if o == 0:
                        recvb[0, c, b] = rv[b, slot]
                    else:
                        sendb[o, c, b] = rv[b, slot]
            for b in range(3):
                for i in range(2):
                    o = 2 * t + i
                    if o:
                        pltpu.make_async_remote_copy(
                            src_ref=sendb.at[o, c, b], dst_ref=recvb.at[o, c, b],
                            send_sem=rsend, recv_sem=rrecv.at[t],
                            device_id={"sec": partner(t, i)}, device_id_type=MESH,
                        ).start()

    def left_products():
        def body(k, carry):
            a = lslot[k]
            stacked = jnp.concatenate([lv[b, a] for b in range(3)], axis=0)
            vectors = jnp.concatenate([tv[0, k], tv[1, k]], axis=1)
            product = jnp.dot(stacked, vectors, preferred_element_type=F32).astype(BF16)
            for b in range(3):
                for v in range(2):
                    xb[k, b, v * 128 : (v + 1) * 128, :] = product[
                        b * 128 : (b + 1) * 128, v * 128 : (v + 1) * 128
                    ]
            return carry

        lax.fori_loop(0, 24, body, 0)

    def right_products(t):
        landed = recvb.at[pl.ds(2 * t, 2)] if t else recvb.at[1]
        pltpu.make_async_copy(landed, landed, rrecv.at[t]).wait()

        def body(q, carry):
            i, c = q // 2, q % 2
            k = ktab_s[c, partner(t, i)]
            at = jnp.maximum(k, 0)
            o = 2 * t + i
            xs = jnp.concatenate([xb[at, b] for b in range(3)], axis=1)
            rs = jnp.concatenate([recvb[o, c, b] for b in range(3)], axis=1)
            value = lax.dot_general(xs, rs, (((1,), (1,)), ((), ())), preferred_element_type=F32)
            value = jnp.where(k >= 0, value, 0.0).astype(BF16)
            for v in range(2):
                for p in range(planes):
                    row = v * 128 + p * 16
                    part[t, p, q * 2 + v] = value[row : row + 16]
            return carry

        lax.fori_loop(0, 4, body, 0)

    def hop(t, step, way):
        back = 4 - step if way == 0 else step - 3
        piece = (z + planes - back * depth) % planes
        to = (z + planes + (depth if way else -depth)) % planes
        return piece, pltpu.make_async_remote_copy(
            src_ref=part.at[t, piece], dst_ref=ring.at[t, step, way],
            send_sem=gsend, recv_sem=grecv.at[t, step],
            device_id={"mpo": to}, device_id_type=MESH,
        )

    def ring_step(t, step):
        ways = range(2 if step < 3 else 1)
        if step:
            landed = ring.at[t, step - 1]
            pltpu.make_async_copy(landed, landed, grecv.at[t, step - 1]).wait()
        for way in ways:
            piece, copy = hop(t, step, way)
            if step:
                part[t, piece] = (
                    part[t, piece].astype(F32) + ring[t, step - 1, way].astype(F32)
                ).astype(BF16)
            copy.start()

    def across(t, i):
        o = 2 * t + i
        return pltpu.make_async_remote_copy(
            src_ref=total.at[t, pl.ds(4 * i, 4)], dst_ref=crossed.at[o],
            send_sem=csend, recv_sem=crecv.at[t],
            device_id={"sec": partner(t, i)}, device_id_type=MESH,
        )

    def finish_sum(t):
        pltpu.make_async_copy(ring.at[t, 3, 0], ring.at[t, 3, 0], grecv.at[t, 3]).wait()
        done = (
            part[t, z].astype(F32) + ring[t, 3, 0].astype(F32) + ring[t, 2, 1].astype(F32)
        ).astype(BF16)
        total[t] = done
        for i in range(2):
            if (t, i) == (0, 0):
                crossed[0] = done[0:4]
            else:
                across(t, i).start()

    def place(t, i):
        source = partner(t, i)
        to, w = source // 4, source % 4
        src = crossed.at[2 * t + i]
        return to, pltpu.make_async_remote_copy(
            src_ref=src, dst_ref=out.at[pl.ds(4 * w, 4), pl.ds(16 * z, 16)],
            send_sem=zsend, recv_sem=zrecv,
            device_id={"mpo": to}, device_id_type=MESH,
        ), pltpu.make_async_copy(
            src, out.at[pl.ds(4 * w, 4), pl.ds(16 * z, 16)], zrecv
        )

    def place_rows(t):
        landed = crossed.at[pl.ds(2 * t, 2)] if t else crossed.at[1]
        pltpu.make_async_copy(landed, landed, crecv.at[t]).wait()
        for i in range(2):
            to, remote, own = place(t, i)

            @pl.when(to == z)
            def _():
                own.start()

            @pl.when(to != z)
            def _():
                remote.start()

    for t in range(AHEAD):
        send_chunk(t)
    loads[1].wait()
    loads[2].wait()
    left_products()
    for turn in range(CHUNKS + LAGS[5]):
        if 0 <= turn - LAGS[5] < CHUNKS:
            place_rows(turn - LAGS[5])
        if 0 <= turn - LAGS[4] < CHUNKS:
            finish_sum(turn - LAGS[4])
        for step in (3, 2, 1):
            if 0 <= turn - LAGS[step] < CHUNKS:
                ring_step(turn - LAGS[step], step)
        if turn < CHUNKS:
            if turn + AHEAD < CHUNKS:
                send_chunk(turn + AHEAD)
            right_products(turn)
            ring_step(turn, 0)

    for sent, sem in (
        (itab.at[pl.ds(1, 31)], isend),
        (sendb.at[pl.ds(1, 31)], rsend),
        (part.at[:, pl.ds(0, 7)], gsend),
        (crossed.at[pl.ds(1, 31)], csend),
        (crossed.at[pl.ds(0, 28)], zsend),
        (out, zrecv),
    ):
        pltpu.make_async_copy(sent, sent, sem).wait()


def local(trial, left_env, right_env, left_slot, dest, right_slot):
    anywhere = pl.BlockSpec(memory_space=pl.ANY)
    dma = pltpu.SemaphoreType.DMA
    rows = pl.pallas_call(
        kernel,
        out_shape=jax.ShapeDtypeStruct((16, 128, 128), BF16),
        in_specs=[anywhere] * 6,
        out_specs=anywhere,
        scratch_shapes=[
            pltpu.VMEM((2, 24, 128, 128), BF16),
            pltpu.VMEM((3, 32, 128, 128), BF16),
            pltpu.VMEM((3, 32, 128, 128), BF16),
            pltpu.VMEM((24, 3, 256, 128), BF16),
            pltpu.VMEM((32, 2, 3, 128, 128), BF16),
            pltpu.VMEM((32, 2, 3, 128, 128), BF16),
            pltpu.VMEM((CHUNKS, 8, 8, 16, 128), BF16),
            pltpu.VMEM((CHUNKS, 4, 2, 8, 16, 128), BF16),
            pltpu.VMEM((CHUNKS, 8, 16, 128), BF16),
            pltpu.VMEM((32, 4, 16, 128), BF16),
            pltpu.VMEM((2, 128), jnp.int32),
            pltpu.VMEM((2, 128), jnp.int32),
            pltpu.VMEM((32, 2, 128), jnp.int32),
            pltpu.SMEM((2, 128), jnp.int32),
            pltpu.SMEM((32, 2, 128), jnp.int32),
            pltpu.SMEM((24,), jnp.int32),
            pltpu.SMEM((24, 1), jnp.int32),
            pltpu.SMEM((24,), jnp.int32),
            dma((3,)),
            dma((3,)),
            dma((2,)),
            dma,
            dma,
            dma,
            dma((CHUNKS,)),
            dma,
            dma((CHUNKS, 4)),
            dma,
            dma((CHUNKS,)),
            dma,
            dma,
        ],
        compiler_params=pltpu.CompilerParams(
            collective_id=0, has_side_effects=True, vmem_limit_bytes=60 * 1024 * 1024
        ),
        name="products",
    )(trial, left_env, right_env, left_slot, dest, right_slot)
    return rows.reshape(8, 2, 128, 128)


def solution(mesh):
    placed = (
        P(None, "sec", None, None),
        P("mpo", "sec", None, None),
        P("mpo", "sec", None, None),
        P("sec"),
        P("sec", None),
        P("sec"),
    )
    return jax.shard_map(
        local,
        mesh=mesh,
        in_specs=placed,
        out_specs=P(("sec", "mpo"), None, None, None),
        check_vma=False,
    )
```
